32 devices in a mesh: seq: 16 (over z, x, core), tp: 2 (over y).
Axes of the slice: x: 2, y: 2, z: 4, core: 2. Of those that a mesh axis runs over, the one named last changes fastest.
Arguments:
- queries: float32 [4096, 4096], P(('seq', 'tp')), may hold values from -8 to 8
- keys: float32 [4096, 2048], P(('seq', 'tp')), may hold values from -8 to 8
- values: float32 [4096, 2048], P(('seq', 'tp')), may hold values from -6 to 6
- out_grad: float32 [4096, 4096], P(('seq', 'tp')), may hold values from -6 to 6
- positions: int32 [4096], P('seq'), may hold values from 0 to 2047, as said below
Outputs:
- attended: float32 [4096, 4096], P(('seq', 'tp'))
- grad_queries: float32 [4096, 4096], P(('seq', 'tp'))
- grad_keys: float32 [4096, 2048], P(('seq', 'tp'))
- grad_values: float32 [4096, 2048], P(('seq', 'tp'))
The draws below stay inside these ranges and needn't reach their ends.
Inputs may be any that keep to these rules, and one draw needn't show every extreme that they name: `positions`: each token's position within its document: one more than the token before, except at a document's first token, where it is 0; the slice's first document may have begun before the slice.
All inputs are finite; a program needn't handle non-finite values.
Results may differ from the reference program's by a relative error of at most 0.0005.
Values sent between devices are 32-bit elements; how exact they have to be, the bound alone decides.
A program may use at most 128 MiB of HBM per device.

```python
import jax
import jax.numpy as jnp
from jax import lax

HEADS = 32
KV_HEADS = 16
HEAD_DIM = 128
WINDOW = 1024
TOK_DEV = 256
TOKENS = 4096


def base_field(key, width):
    return jnp.clip(jax.random.normal(key, (TOKENS, width, HEAD_DIM), jnp.float32), -8.0, 8.0)


def draw_queries(key, part):
    base = base_field(jax.random.fold_in(key, 1), HEADS)
    return base.reshape(TOKENS, HEADS * HEAD_DIM).astype(jnp.float32)


def draw_keys(key, part):
    base = base_field(jax.random.fold_in(key, 2), KV_HEADS)
    return base.reshape(TOKENS, KV_HEADS * HEAD_DIM).astype(jnp.float32)


def draw_positions(key, part):
    token_index = jnp.arange(TOKENS, dtype=jnp.int32)
    region_count = (TOKENS + 1023) // 1024
    pick = jax.random.randint(jax.random.fold_in(key, 21), (region_count,), 0, 4)
    spacing_table = jnp.array([32, 256, 2048, 16384], jnp.int32)
    spacing = spacing_table[pick][token_index // 1024]
    raw_draw = jax.random.randint(jax.random.fold_in(key, 22), (TOKENS,), 0, 2 ** 30)
    is_start = (raw_draw % spacing == 0) & (token_index < TOKENS // 2)
    is_start = is_start | (token_index == TOKENS // 2) | (token_index == TOKENS // 4)
    is_start = is_start & (token_index > 0)
    doc_start = lax.cummax(jnp.where(is_start, token_index, 0))
    offset = jax.random.randint(jax.random.fold_in(key, 23), (), 0, TOKENS // 4)
    return (token_index - doc_start + jnp.where(doc_start == 0, offset, 0)).astype(jnp.int32)


def steps_of(own_key, extent, cuts, low, largest):
    def one(position, shards_of):
        steps = jax.random.uniform(jax.random.fold_in(jax.random.fold_in(own_key, 6), position), (shards_of,), jnp.float32, low / len(cuts), largest / len(cuts))
        return jnp.repeat(jnp.exp(steps), extent[position] // shards_of).reshape((-1,) + (1,) * (len(extent) - position - 1))

    factor_of = one(*cuts[0])
    for cut in cuts[1:]:
        factor_of = factor_of * one(*cut)
    return factor_of


def centred(own_key, dims, scale, reach, pieces=(), held_as=jnp.bfloat16):
    drawn = scale * jax.random.normal(own_key, dims, jnp.float32)
    if pieces:
        drawn = drawn * steps_of(own_key, dims, pieces, -0.22, 0.18)
    return jnp.clip(drawn, -reach, reach).astype(held_as)


def setup_inputs(seed: int = 0) -> dict:
    splits = jax.random.split(jax.random.key(seed), 6)
    queries = draw_queries(jax.random.fold_in(splits[5], 71), 0)
    keys = draw_keys(jax.random.fold_in(splits[5], 71), 0)
    values = centred(splits[2], (TOKENS, KV_HEADS * HEAD_DIM), 1.0, 6.0, ((0, 32),), jnp.float32)
    out_grad = centred(splits[3], (TOKENS, HEADS * HEAD_DIM), 1.0, 6.0, ((0, 32),), jnp.float32)
    positions = draw_positions(jax.random.fold_in(splits[5], 71), 0)
    return {"queries": queries, "keys": keys, "values": values, "out_grad": out_grad, "positions": positions}


score_scale = 168.0 ** (-0.5)
neg_fill = -1e+30

def reference(queries, keys, values, out_grad, positions):
    total_rows = queries.shape[0]
    group_size = HEADS // KV_HEADS
    token_index = jnp.arange(total_rows, dtype=jnp.int32)
    doc_starts = (token_index - positions.astype(jnp.int32)).astype(jnp.int32)
    padded_starts = jnp.concatenate([jnp.zeros((WINDOW,), jnp.int32), doc_starts])
    block_count = total_rows // TOK_DEV
    precise = lax.Precision.HIGHEST

    def forward(query_all, key_all, value_all):
        padded_keys = jnp.concatenate([jnp.zeros((WINDOW, key_all.shape[1]), key_all.dtype), key_all])
        padded_values = jnp.concatenate([jnp.zeros((WINDOW, value_all.shape[1]), value_all.dtype), value_all])

        def attend_block(block_id):
            block_start = (block_id * TOK_DEV).astype(jnp.int32)
            query_block = lax.dynamic_slice_in_dim(query_all, block_start, TOK_DEV, 0).reshape(TOK_DEV, KV_HEADS, group_size, HEAD_DIM)
            key_block = lax.dynamic_slice_in_dim(padded_keys, block_start, WINDOW + TOK_DEV, 0).reshape(WINDOW + TOK_DEV, KV_HEADS, HEAD_DIM)
            value_block = lax.dynamic_slice_in_dim(padded_values, block_start, WINDOW + TOK_DEV, 0).reshape(WINDOW + TOK_DEV, KV_HEADS, HEAD_DIM)
            query_starts = lax.dynamic_slice_in_dim(doc_starts, block_start, TOK_DEV, 0)
            key_starts = lax.dynamic_slice_in_dim(padded_starts, block_start, WINDOW + TOK_DEV, 0)
            query_index = block_start + jnp.arange(TOK_DEV, dtype=jnp.int32)
            key_index = block_start - WINDOW + jnp.arange(WINDOW + TOK_DEV, dtype=jnp.int32)
            offsets = query_index[:, None] - key_index[None, :]
            visible = (key_index >= 0)[None, :] & (offsets >= 0) & (offsets < WINDOW) & (query_starts[:, None] == key_starts[None, :])
            scores = jnp.einsum('qgrd,kgd->grqk', query_block, key_block, precision=precise) * score_scale
            scores = jnp.where(visible, scores, neg_fill)
            top_score = lax.stop_gradient(lax.optimization_barrier(jnp.max(scores, axis=-1, keepdims=True)))
            weights = jnp.exp(scores - top_score)
            totals = lax.optimization_barrier(jnp.sum(weights, axis=-1))
            mixed = jnp.einsum('grqk,kgd->qgrd', weights, value_block, precision=precise)
            mixed = mixed / jnp.transpose(totals, (2, 0, 1))[..., None]
            return mixed.reshape(TOK_DEV, HEADS * HEAD_DIM)
        results = lax.map(jax.checkpoint(attend_block), jnp.arange(block_count, dtype=jnp.int32))
        return results.reshape(total_rows, HEADS * HEAD_DIM)
    attended, pullback = jax.vjp(forward, queries, keys, values)
    grad_queries, grad_keys, grad_values = pullback(out_grad)
    return (attended, grad_queries, grad_keys, grad_values)
```

```python
import functools

import jax
import jax.numpy as jnp
from jax import lax
from jax.experimental import pallas as pl
from jax.experimental.pallas import tpu as pltpu
from jax.sharding import PartitionSpec as P

HEAD_DIM = 128
WINDOW = 1024
CHUNKS = 2

score_scale = 168.0 ** (-0.5)
neg_fill = -1e30
f32 = jnp.float32
bf16 = jnp.bfloat16


def split(x):
    hi = x.astype(bf16)
    lo = (x - hi.astype(f32)).astype(bf16)
    return hi, lo


def mm(a, b, dims):
    return lax.dot_general(a, b, (dims, ((), ())), preferred_element_type=f32)


NT = ((1,), (1,))
NN = ((1,), (0,))
TN = ((0,), (0,))


def attend(reach1, group, low_ref, pos_ref, kidx_ref, q_ref, g_ref, *refs):
    k_refs = refs[:reach1]
    v_refs = refs[reach1 : 2 * reach1]
    o_ref, dq_ref = refs[2 * reach1 : 2 * reach1 + 2]
    dk_refs = refs[2 * reach1 + 2 : 3 * reach1 + 2]
    dv_refs = refs[3 * reach1 + 2 : 4 * reach1 + 2]
    s_ref, ph_ref, pl_ref = refs[4 * reach1 + 2 :]
    d = HEAD_DIM
    tok = q_ref.shape[0]

    def stacked(ref):
        return jnp.concatenate([ref[:, r * d : (r + 1) * d] for r in range(group)], axis=0)

    low = jnp.concatenate([low_ref[...]] * group, axis=0)
    pos = jnp.concatenate([pos_ref[...]] * group, axis=0)
    q = stacked(q_ref) * score_scale
    qh, ql = split(q)
    qhl = jnp.concatenate([qh, ql], axis=1)
    top = None
    for j in range(reach1):
        kh, kl = split(k_refs[j][...])
        s = mm(qhl, jnp.concatenate([kh, kh], axis=1), NT) + mm(qh, kl, NT)
        kid = kidx_ref[j : j + 1, :]
        s = jnp.where((kid >= low) & (kid <= pos), s, neg_fill)
        s_ref[j] = s
        m = jnp.max(s, axis=1, keepdims=True)
        top = m if top is None else jnp.maximum(top, m)
    total = jnp.zeros_like(top)
    acc = jnp.zeros((group * tok, d), f32)
    for j in range(reach1):
        p = jnp.exp(s_ref[j] - top)
        total = total + jnp.sum(p, axis=1, keepdims=True)
        ph, plo = split(p)
        ph_ref[j] = ph
        pl_ref[j] = plo
        vh, vl = split(v_refs[j][...])
        both = mm(ph, jnp.concatenate([vh, vl], axis=1), NN)
        acc = acc + (both[:, :d] + both[:, d:]) + mm(plo, vh, NN)
    inv = 1.0 / total
    out = acc * inv
    for r in range(group):
        o_ref[:, r * d : (r + 1) * d] = out[r * tok : (r + 1) * tok]
    grad = stacked(g_ref) * inv
    delta = jnp.sum(grad * out, axis=1, keepdims=True)
    gh, gl = split(grad)
    ghl = jnp.concatenate([gh, gl], axis=1)
    dq = jnp.zeros((group * tok, d), f32)
    for j in range(reach1):
        vh, vl = split(v_refs[j][...])
        kh, kl = split(k_refs[j][...])
        ph, plo = ph_ref[j], pl_ref[j]
        dp = mm(ghl, jnp.concatenate([vh, vh], axis=1), NT) + mm(gh, vl, NT)
        ds = (ph.astype(f32) + plo.astype(f32)) * (dp - delta)
        both = mm(ph, ghl, TN)
        dv_refs[j][...] = both[:, :d] + both[:, d:] + mm(plo, gh, TN)
        sh, sl = split(ds)
        both = mm(sh, qhl, TN)
        dk_refs[j][...] = both[:, :d] + both[:, d:] + mm(sl, qh, TN)
        both = mm(sh, jnp.concatenate([kh, kl], axis=1), NN)
        dq = dq + (both[:, :d] + both[:, d:]) + mm(sl, kh, NN)
    dq = dq * score_scale
    for r in range(group):
        dq_ref[:, r * d : (r + 1) * d] = dq[r * tok : (r + 1) * tok]


def run_attend(low, pos, kidx, q, grad, kv_pieces):
    tok = q.shape[0]
    reach1 = len(kv_pieces)
    kv_cols = kv_pieces[0].shape[1] // 2
    heads = kv_cols // HEAD_DIM
    group = q.shape[1] // kv_cols
    d = HEAD_DIM
    whole = lambda *shape: pl.BlockSpec(shape, lambda h: (0,) * len(shape))
    qspec = pl.BlockSpec((tok, group * d), lambda h: (0, h))
    kspec = pl.BlockSpec((tok, d), lambda h: (0, h))
    vspec = pl.BlockSpec((tok, d), lambda h: (0, h + heads))
    flops = 2 * 6 * 3 * tok * group * tok * reach1 * d * heads
    outs = pl.pallas_call(
        functools.partial(attend, reach1, group),
        grid=(heads,),
        in_specs=[whole(tok, 1), whole(tok, 1), whole(*kidx.shape), qspec, qspec]
        + [kspec] * reach1
        + [vspec] * reach1,
        out_specs=[qspec, qspec] + [kspec] * (2 * reach1),
        out_shape=[jax.ShapeDtypeStruct(q.shape, f32)] * 2
        + [jax.ShapeDtypeStruct((tok, kv_cols), f32)] * (2 * reach1),
        scratch_shapes=[
            pltpu.VMEM((reach1, group * tok, tok), f32),
            pltpu.VMEM((reach1, group * tok, tok), bf16),
            pltpu.VMEM((reach1, group * tok, tok), bf16),
        ],
        compiler_params=pltpu.CompilerParams(vmem_limit_bytes=40 * 2**20),
        cost_estimate=pl.CostEstimate(
            flops=2 * flops, bytes_accessed=4 * (4 * q.size + 20 * tok * kv_cols), transcendentals=0
        ),
    )(low, pos, kidx, q, grad, *kv_pieces, *kv_pieces)
    return outs[0], outs[1], outs[2 : 2 + reach1], outs[2 + reach1 :]


def per_device(queries, keys, values, out_grad, positions):
    seq_size, tp_size = lax.axis_size("seq"), lax.axis_size("tp")
    s = lax.axis_index("seq")
    t = lax.axis_index("tp")
    rows = queries.shape[0]
    tok = rows * tp_size
    pair = tp_size == 2
    kv_local = keys.shape[1] // tp_size
    q_local = queries.shape[1] // tp_size
    chunks = CHUNKS if pair else 1
    kw, qw = kv_local // chunks, q_local // chunks

    def shift_seq(x, route):
        return lax.ppermute(x, "seq", [(a, b) for a, b in route if 0 <= b < seq_size])

    up = [(i, i + 4) for i in range(seq_size)]
    down = [(i, i - 4) for i in range(seq_size)]
    cross = [(i, i ^ 2) for i in range(seq_size)]
    core = [(i, i ^ 1) for i in range(seq_size)]
    swap = [(0, 1), (1, 0)]

    local = jnp.arange(tok, dtype=jnp.int32)
    if pair:
        local = lax.rem(local + t * rows, tok)
        mine, other = positions[:rows], positions[rows:]
        positions = jnp.where(t == 0, positions, jnp.concatenate([other, mine]))
    first = s * tok
    pos = first + local
    low = jnp.maximum(jnp.maximum(pos - positions, pos - (WINDOW - 1)), 0)

    b = s % 4
    base = s - b
    x1, c1 = b // 2 == 1, b % 2 == 1
    p2_block = jnp.where(x1, s - 2, s - 2)
    c_p2 = (s ^ 1) - 2
    c_first = jnp.where(c1, s - 1, s - 3)
    blocks = jnp.stack([s, s - 4, p2_block, c_first, c_p2])
    kidx = blocks[:, None] * tok + local[None, :]

    pos, low = pos[:, None], low[:, None]

    results = []
    for c in range(chunks):
        if pair:
            def part(x, width, who):
                return lax.dynamic_slice_in_dim(x, who * width * chunks + c * width, width, 1)

            def pack(who):
                return jnp.concatenate(
                    [part(queries, qw, who), part(out_grad, qw, who), part(keys, kw, who), part(values, kw, who)],
                    axis=1,
                )

            packed = jnp.concatenate([pack(t), lax.ppermute(pack(1 - t), "tp", swap)], axis=0)
            q, grad, own = packed[:, :qw], packed[:, qw : 2 * qw], packed[:, 2 * qw :]
        else:
            a2a = lambda x: lax.all_to_all(x, "tp", split_axis=1, concat_axis=0, tiled=True)
            q, grad = a2a(queries), a2a(out_grad)
            own = jnp.concatenate([a2a(keys), a2a(values)], axis=1)
        prior = shift_seq(own, up)
        crossed = shift_seq(jnp.where(x1, prior, own), cross)
        near = shift_seq(jnp.where(c1, prior, own), core)
        near_crossed = shift_seq(crossed, core)
        pieces = [own, prior, crossed, near, near_crossed]
        out, dq, dks, dvs = run_attend(low, pos, kidx, q, grad, pieces)
        g_own, g_prior, g_crossed, g_near, g_nc = [
            jnp.concatenate([dk, dv], axis=1) for dk, dv in zip(dks, dvs)
        ]
        near_back = shift_seq(g_near, core)
        g_crossed = g_crossed + shift_seq(g_nc, core)
        zero = jnp.zeros_like(g_own)
        g_own = g_own + jnp.where(c1, zero, near_back)
        g_prior = g_prior + jnp.where(c1, near_back, zero)
        cross_back = shift_seq(g_crossed, cross)
        g_own = g_own + jnp.where(x1, zero, cross_back)
        g_prior = g_prior + jnp.where(x1, cross_back, zero)
        g_own = g_own + shift_seq(g_prior, down)
        if pair:
            full = jnp.concatenate([out, dq, g_own], axis=1)
            results.append((full[:rows], lax.ppermute(full[rows:], "tp", swap)))
        else:
            b2a = lambda x: lax.all_to_all(x, "tp", split_axis=0, concat_axis=1, tiled=True)
            return (b2a(out), b2a(dq), b2a(g_own[:, :kw]), b2a(g_own[:, kw:]))

    def gather(begin, width):
        mine = jnp.concatenate([r[0][:, begin : begin + width] for r in results], axis=1)
        theirs = jnp.concatenate([r[1][:, begin : begin + width] for r in results], axis=1)
        return jnp.where(
            t == 0,
            jnp.concatenate([mine, theirs], axis=1),
            jnp.concatenate([theirs, mine], axis=1),
        )

    return (
        gather(0, qw),
        gather(qw, qw),
        gather(2 * qw, kw),
        gather(2 * qw + kw, kw),
    )


def solution(mesh):
    spec = P(("seq", "tp"), None)
    return jax.shard_map(
        per_device,
        mesh=mesh,
        in_specs=(spec, spec, spec, spec, P("seq")),
        out_specs=(spec, spec, spec, spec),
        check_vma=False,
    )
```

```python
import functools

import jax
import jax.numpy as jnp
from jax import lax
from jax.experimental import pallas as pl
from jax.experimental.pallas import tpu as pltpu
from jax.sharding import PartitionSpec as P

HEAD_DIM = 128
WINDOW = 1024
LEAD = 5
MESH = pl.DeviceIdType.MESH

score_scale = 168.0 ** (-0.5)
neg_fill = -1e30
f32 = jnp.float32
bf16 = jnp.bfloat16


def split(x):
    hi = x.astype(bf16)
    lo = (x - hi.astype(f32)).astype(bf16)
    return hi, lo


def mm(a, b, dims):
    return lax.dot_general(a, b, (dims, ((), ())), preferred_element_type=f32)


NT = ((1,), (1,))
NN = ((1,), (0,))
TN = ((0,), (0,))


def attend(reach1, group, low_ref, pos_ref, kidx_ref, q_ref, g_ref, *refs):
    k_refs = refs[:reach1]
    v_refs = refs[reach1 : 2 * reach1]
    o_ref, dq_ref = refs[2 * reach1 : 2 * reach1 + 2]
    dk_refs = refs[2 * reach1 + 2 : 3 * reach1 + 2]
    dv_refs = refs[3 * reach1 + 2 : 4 * reach1 + 2]
    s_ref, ph_ref, pl_ref = refs[4 * reach1 + 2 :]
    d = HEAD_DIM
    tok = q_ref.shape[0]

    def stacked(ref):
        return jnp.concatenate([ref[:, r * d : (r + 1) * d] for r in range(group)], axis=0)

    low = jnp.concatenate([low_ref[...]] * group, axis=0)
    pos = jnp.concatenate([pos_ref[...]] * group, axis=0)
    q = stacked(q_ref) * score_scale
    qh, ql = split(q)
    qhl = jnp.concatenate([qh, ql], axis=1)
    top = None
    for j in range(reach1):
        kh, kl = split(k_refs[j][...])
        s = mm(qhl, jnp.concatenate([kh, kh], axis=1), NT) + mm(qh, kl, NT)
        kid = kidx_ref[j : j + 1, :]
        s = jnp.where((kid >= low) & (kid <= pos), s, neg_fill)
        s_ref[j] = s
        m = jnp.max(s, axis=1, keepdims=True)
        top = m if top is None else jnp.maximum(top, m)
    total = jnp.zeros_like(top)
    acc = jnp.zeros((group * tok, d), f32)
    for j in range(reach1):
        p = jnp.exp(s_ref[j] - top)
        total = total + jnp.sum(p, axis=1, keepdims=True)
        ph, plo = split(p)
        ph_ref[j] = ph
        pl_ref[j] = plo
        vh, vl = split(v_refs[j][...])
        both = mm(ph, jnp.concatenate([vh, vl], axis=1), NN)
        acc = acc + (both[:, :d] + both[:, d:]) + mm(plo, vh, NN)
    inv = 1.0 / total
    out = acc * inv
    for r in range(group):
        o_ref[:, r * d : (r + 1) * d] = out[r * tok : (r + 1) * tok]
    grad = stacked(g_ref) * inv
    delta = jnp.sum(grad * out, axis=1, keepdims=True)
    gh, gl = split(grad)
    ghl = jnp.concatenate([gh, gl], axis=1)
    dq = jnp.zeros((group * tok, d), f32)
    for j in range(reach1):
        vh, vl = split(v_refs[j][...])
        kh, kl = split(k_refs[j][...])
        ph, plo = ph_ref[j], pl_ref[j]
        dp = mm(ghl, jnp.concatenate([vh, vh], axis=1), NT) + mm(gh, vl, NT)
        ds = (ph.astype(f32) + plo.astype(f32)) * (dp - delta)
        both = mm(ph, ghl, TN)
        dv_refs[j][...] = both[:, :d] + both[:, d:] + mm(plo, gh, TN)
        sh, sl = split(ds)
        both = mm(sh, qhl, TN)
        dk_refs[j][...] = both[:, :d] + both[:, d:] + mm(sl, qh, TN)
        both = mm(sh, jnp.concatenate([kh, kl], axis=1), NN)
        dq = dq + (both[:, :d] + both[:, d:]) + mm(sl, kh, NN)
    dq = dq * score_scale
    for r in range(group):
        dq_ref[:, r * d : (r + 1) * d] = dq[r * tok : (r + 1) * tok]


def run_attend(low, pos, kidx, q, grad, kv_pieces):
    tok = q.shape[0]
    reach1 = len(kv_pieces)
    kv_cols = kv_pieces[0].shape[1] // 2
    heads = kv_cols // HEAD_DIM
    group = q.shape[1] // kv_cols
    d = HEAD_DIM
    whole = lambda *shape: pl.BlockSpec(shape, lambda h: (0,) * len(shape))
    qspec = pl.BlockSpec((tok, group * d), lambda h: (0, h))
    kspec = pl.BlockSpec((tok, d), lambda h: (0, h))
    vspec = pl.BlockSpec((tok, d), lambda h: (0, h + heads))
    flops = 2 * 6 * 3 * tok * group * tok * reach1 * d * heads
    outs = pl.pallas_call(
        functools.partial(attend, reach1, group),
        grid=(heads,),
        in_specs=[whole(tok, 1), whole(tok, 1), whole(*kidx.shape), qspec, qspec]
        + [kspec] * reach1
        + [vspec] * reach1,
        out_specs=[qspec, qspec] + [kspec] * (2 * reach1),
        out_shape=[jax.ShapeDtypeStruct(q.shape, f32)] * 2
        + [jax.ShapeDtypeStruct((tok, kv_cols), f32)] * (2 * reach1),
        scratch_shapes=[
            pltpu.VMEM((reach1, group * tok, tok), f32),
            pltpu.VMEM((reach1, group * tok, tok), bf16),
            pltpu.VMEM((reach1, group * tok, tok), bf16),
        ],
        compiler_params=pltpu.CompilerParams(vmem_limit_bytes=40 * 2**20),
        cost_estimate=pl.CostEstimate(
            flops=2 * flops, bytes_accessed=4 * (4 * q.size + 20 * tok * kv_cols), transcendentals=0
        ),
    )(low, pos, kidx, q, grad, *kv_pieces, *kv_pieces)
    return outs[0], outs[1], outs[2 : 2 + reach1], outs[2 + reach1 :]


def fused(heads, group, n, low_ref, pos_ref, kidx_ref, q_hbm, k_hbm, v_hbm, g_hbm, o_hbm, dq_hbm, dk_hbm, dv_hbm,
          qb, gb, kv, dkv, ob, dqb, r34, rx, rd, s_ref, ph_ref, pl_ref,
          in_send, in_recv, in_local, up_send, up_recv, cross_send, cross_recv, core_send, core_recv,
          b34_send, b34_recv, bx_send, bx_recv, bd_send, bd_recv, out_send, out_recv, out_local):
    d = HEAD_DIM
    gd = group * d
    s, t = lax.axis_index("seq"), lax.axis_index("tp")
    rows = q_hbm.shape[0]
    c1 = lax.rem(s, 2)
    x1 = lax.rem(s // 2, 2)
    mate = {"tp": 1 - t}
    core = {"seq": s + 1 - 2 * c1}
    cross = {"seq": s + 2 - 4 * x1}
    above = {"seq": lax.rem(s + 4, n)}
    below = {"seq": lax.rem(s + n - 4, n)}
    has_below, has_above = s >= 4, s < n - 4

    barrier = pltpu.get_barrier_semaphore()

    def greet(who):
        pl.semaphore_signal(barrier, inc=1, device_id=who, device_id_type=MESH)

    for who in (mate, core, cross, above, below):
        greet(who)
    pl.semaphore_wait(barrier, 5)

    def remote(a, b, ss, rs, who):
        return pltpu.make_async_remote_copy(
            src_ref=a, dst_ref=b, send_sem=ss, recv_sem=rs, device_id=who, device_id_type=MESH
        )

    def cols(ref, who, h, width):
        start = pl.multiple_of(who * (heads * width) + h * width, width)
        return ref.at[:, pl.ds(start, width)]

    def landing(i, h, half):
        r = pl.ds(half * rows, rows)
        if i == 0:
            return kv.at[h, 0, 0, r, :]
        if i == 1:
            return kv.at[h, 0, 1, r, :]
        return (qb if i == 2 else gb).at[h, r, :]

    in_src = ((k_hbm, d), (v_hbm, d), (q_hbm, gd), (g_hbm, gd))

    def y_in(i, h):
        ref, w = in_src[i]
        return remote(cols(ref, 1 - t, h, w), landing(i, h, 1), in_send.at[i, h], in_recv.at[i, h], mate)

    def l_in(i, h):
        ref, w = in_src[i]
        return pltpu.make_async_copy(cols(ref, t, h, w), landing(i, h, 0), in_local.at[i, h])

    def up(h):
        return remote(kv.at[h, 0], kv.at[h, 1], up_send.at[h], up_recv.at[h], above)

    def over(h):
        return remote(kv.at[h, x1], kv.at[h, 2], cross_send.at[h], cross_recv.at[h], cross)

    def near(i, h):
        a = kv.at[h, c1] if i == 0 else kv.at[h, 2]
        return remote(a, kv.at[h, 3 + i], core_send.at[i, h], core_recv.at[i, h], core)

    def b34(h):
        return remote(dkv.at[h, pl.ds(3, 2)], r34.at[h], b34_send.at[h], b34_recv.at[h], core)

    def bx(h):
        return remote(dkv.at[h, 2], rx.at[h], bx_send.at[h], bx_recv.at[h], cross)

    def bd(h):
        return remote(dkv.at[h, 1], rd.at[h], bd_send.at[h], bd_recv.at[h], below)

    out_dst = ((o_hbm, gd), (dq_hbm, gd), (dk_hbm, d), (dv_hbm, d))

    def leaving(i, h, half):
        r = pl.ds(half * rows, rows)
        if i < 2:
            return (ob if i == 0 else dqb).at[h, r, :]
        return dkv.at[h, 0, i - 2, r, :]

    def y_out(i, h):
        ref, w = out_dst[i]
        return remote(leaving(i, h, 1), cols(ref, t, h, w), out_send.at[i, h], out_recv.at[i, h], mate)

    def l_out(i, h):
        ref, w = out_dst[i]
        return pltpu.make_async_copy(leaving(i, h, 0), cols(ref, t, h, w), out_local.at[i, h])

    def each(body):
        def run(h, carry):
            body(h)
            return carry

        lax.fori_loop(0, heads, run, 0)

    def begin(kinds):
        def body(h):
            for i in kinds:
                y_in(i, h).start()
                l_in(i, h).start()

        each(body)

    begin((0, 1))
    begin((2, 3))

    def stage_a(h):
        for i in (0, 1):
            l_in(i, h).wait()
            y_in(i, h).wait_recv()

        @pl.when(has_above)
        def _():
            up(h).start()

    def stage_b(h):
        @pl.when(has_below)
        def _():
            up(h).wait_recv()

        @pl.when(jnp.logical_not(has_below))
        def _():
            kv[h, 1] = jnp.zeros(kv.shape[2:], f32)

        over(h).start()
        near(0, h).start()

    def stage_c(h):
        over(h).wait_recv()
        near(1, h).start()

    def compute(h):
        for i in (2, 3):
            l_in(i, h).wait()
            y_in(i, h).wait_recv()
        for i in (0, 1):
            near(i, h).wait_recv()
        attend(
            5, group, low_ref, pos_ref, kidx_ref, qb.at[h], gb.at[h],
            *[kv.at[h, j, 0] for j in range(5)],
            *[kv.at[h, j, 1] for j in range(5)],
            ob.at[h], dqb.at[h],
            *[dkv.at[h, j, 0] for j in range(5)],
            *[dkv.at[h, j, 1] for j in range(5)],
            s_ref, ph_ref, pl_ref,
        )
        b34(h).start()
        for i in (0, 1):
            y_out(i, h).start()
            l_out(i, h).start()

    def stage_e2(h):
        b34(h).wait()
        dkv[h, 2] = dkv[h, 2] + r34[h, 1]
        dkv[h, c1] = dkv[h, c1] + r34[h, 0]
        bx(h).start()

    def stage_e3(h):
        bx(h).wait()
        dkv[h, x1] = dkv[h, x1] + rx[h]

        @pl.when(has_below)
        def _():
            bd(h).start()

    def stage_e4(h):
        @pl.when(has_above)
        def _():
            bd(h).wait_recv()
            dkv[h, 0] = dkv[h, 0] + rd[h]

        for i in (2, 3):
            y_out(i, h).start()
            l_out(i, h).start()

    stages = STAGES(stage_a, stage_b, stage_c, compute, stage_e2, stage_e3, stage_e4)
    last = max(lag for lag, _ in stages)

    def step(i, carry):
        for lag, stage in stages:
            @pl.when((i >= lag) & (i < lag + heads))
            def _():
                stage(i - lag)

        return carry

    lax.fori_loop(0, heads + last, step, 0)

    def finish(h):
        for i in range(4):
            y_in(i, h).wait_send()
            y_out(i, h).wait()
            l_out(i, h).wait()
        over(h).wait_send()
        near(0, h).wait_send()
        near(1, h).wait_send()

        @pl.when(has_above)
        def _():
            up(h).wait_send()

        @pl.when(has_below)
        def _():
            bd(h).wait_send()

    each(finish)


def STAGES(a, b, c, compute, e2, e3, e4):
    return ((0, a), (1, b), (2, c), (LEAD, compute), (LEAD + 1, e2), (LEAD + 2, e3), (LEAD + 3, e4))


def run_fused(low, pos, kidx, queries, keys, values, out_grad):
    rows = queries.shape[0]
    tok = 2 * rows
    d = HEAD_DIM
    heads = keys.shape[1] // (2 * d)
    group = queries.shape[1] // keys.shape[1]
    gd = group * d
    n = lax.axis_size("seq")
    vm = pl.BlockSpec(memory_space=pltpu.VMEM)
    hbm = pl.BlockSpec(memory_space=pl.ANY)
    dma = lambda *shape: pltpu.SemaphoreType.DMA(shape)
    flops = 2 * 6 * 3 * tok * group * tok * 5 * d * heads
    return pl.pallas_call(
        functools.partial(fused, heads, group, n),
        in_specs=[vm] * 3 + [hbm] * 4,
        out_specs=[hbm] * 4,
        out_shape=[jax.ShapeDtypeStruct(x.shape, f32) for x in (queries, queries, keys, values)],
        scratch_shapes=[
            pltpu.VMEM((heads, tok, gd), f32),
            pltpu.VMEM((heads, tok, gd), f32),
            pltpu.VMEM((heads, 5, 2, tok, d), f32),
            pltpu.VMEM((heads, 5, 2, tok, d), f32),
            pltpu.VMEM((heads, tok, gd), f32),
            pltpu.VMEM((heads, tok, gd), f32),
            pltpu.VMEM((heads, 2, 2, tok, d), f32),
            pltpu.VMEM((heads, 2, tok, d), f32),
            pltpu.VMEM((heads, 2, tok, d), f32),
            pltpu.VMEM((5, group * tok, tok), f32),
            pltpu.VMEM((5, group * tok, tok), bf16),
            pltpu.VMEM((5, group * tok, tok), bf16),
            dma(4, heads), dma(4, heads), dma(4, heads),
            dma(heads), dma(heads),
            dma(heads), dma(heads),
            dma(2, heads), dma(2, heads),
            dma(heads), dma(heads),
            dma(heads), dma(heads),
            dma(heads), dma(heads),
            dma(4, heads), dma(4, heads), dma(4, heads),
        ],
        compiler_params=pltpu.CompilerParams(
            vmem_limit_bytes=58 * 2**20, collective_id=0, has_side_effects=True
        ),
        cost_estimate=pl.CostEstimate(flops=flops, bytes_accessed=48 * queries.size, transcendentals=0),
    )(low, pos, kidx, queries, keys, values, out_grad)


def per_device(queries, keys, values, out_grad, positions):
    seq_size, tp_size = lax.axis_size("seq"), lax.axis_size("tp")
    s = lax.axis_index("seq")
    t = lax.axis_index("tp")
    rows = queries.shape[0]
    tok = rows * tp_size
    pair = tp_size == 2
    kw = keys.shape[1] // tp_size

    def shift_seq(x, route):
        return lax.ppermute(x, "seq", [(a, b) for a, b in route if 0 <= b < seq_size])

    up = [(i, i + 4) for i in range(seq_size)]
    down = [(i, i - 4) for i in range(seq_size)]
    cross = [(i, i ^ 2) for i in range(seq_size)]
    core = [(i, i ^ 1) for i in range(seq_size)]

    local = jnp.arange(tok, dtype=jnp.int32)
    if pair:
        local = lax.rem(local + t * rows, tok)
        mine, other = positions[:rows], positions[rows:]
        positions = jnp.where(t == 0, positions, jnp.concatenate([other, mine]))
    first = s * tok
    pos = first + local
    low = jnp.maximum(jnp.maximum(pos - positions, pos - (WINDOW - 1)), 0)

    b = s % 4
    base = s - b
    x1, c1 = b // 2 == 1, b % 2 == 1
    p2_block = s - 2
    c_p2 = (s ^ 1) - 2
    c_first = jnp.where(c1, s - 1, s - 3)
    blocks = jnp.stack([s, s - 4, p2_block, c_first, c_p2])
    kidx = blocks[:, None] * tok + local[None, :]

    pos, low = pos[:, None], low[:, None]
    if pair:
        return tuple(run_fused(low, pos, kidx, queries, keys, values, out_grad))

    a2a = lambda x: lax.all_to_all(x, "tp", split_axis=1, concat_axis=0, tiled=True)
    b2a = lambda x: lax.all_to_all(x, "tp", split_axis=0, concat_axis=1, tiled=True)
    q, grad = a2a(queries), a2a(out_grad)
    own = jnp.concatenate([a2a(keys), a2a(values)], axis=1)
    prior = shift_seq(own, up)
    crossed = shift_seq(jnp.where(x1, prior, own), cross)
    near = shift_seq(jnp.where(c1, prior, own), core)
    near_crossed = shift_seq(crossed, core)
    pieces = [own, prior, crossed, near, near_crossed]
    out, dq, dks, dvs = run_attend(low, pos, kidx, q, grad, pieces)
    g_own, g_prior, g_crossed, g_near, g_nc = [
        jnp.concatenate([dk, dv], axis=1) for dk, dv in zip(dks, dvs)
    ]
    near_back = shift_seq(g_near, core)
    g_crossed = g_crossed + shift_seq(g_nc, core)
    zero = jnp.zeros_like(g_own)
    g_own = g_own + jnp.where(c1, zero, near_back)
    g_prior = g_prior + jnp.where(c1, near_back, zero)
    cross_back = shift_seq(g_crossed, cross)
    g_own = g_own + jnp.where(x1, zero, cross_back)
    g_prior = g_prior + jnp.where(x1, cross_back, zero)
    g_own = g_own + shift_seq(g_prior, down)
    return (b2a(out), b2a(dq), b2a(g_own[:, :kw]), b2a(g_own[:, kw:]))


def solution(mesh):
    spec = P(("seq", "tp"), None)
    return jax.shard_map(
        per_device,
        mesh=mesh,
        in_specs=(spec, spec, spec, spec, P("seq")),
        out_specs=(spec, spec, spec, spec),
        check_vma=False,
    )
```

```python
import functools

import jax
import jax.numpy as jnp
from jax import lax
from jax.experimental import pallas as pl
from jax.experimental.pallas import tpu as pltpu
from jax.sharding import PartitionSpec as P

HEAD_DIM = 128
WINDOW = 1024
LEAD = 5
MESH = pl.DeviceIdType.MESH

score_scale = 168.0 ** (-0.5)
neg_fill = -1e30
f32 = jnp.float32
bf16 = jnp.bfloat16


def split(x):
    hi = x.astype(bf16)
    lo = (x - hi.astype(f32)).astype(bf16)
    return hi, lo


def mm(a, b, dims):
    return lax.dot_general(a, b, (dims, ((), ())), preferred_element_type=f32)


NT = ((1,), (1,))
NN = ((1,), (0,))
TN = ((0,), (0,))


def attend(reach1, group, low_ref, pos_ref, kidx_ref, q_ref, g_ref, *refs):
    k_refs = refs[:reach1]
    v_refs = refs[reach1 : 2 * reach1]
    o_ref, dq_ref = refs[2 * reach1 : 2 * reach1 + 2]
    dk_refs = refs[2 * reach1 + 2 : 3 * reach1 + 2]
    dv_refs = refs[3 * reach1 + 2 : 4 * reach1 + 2]
    s_ref, ph_ref, pl_ref = refs[4 * reach1 + 2 :]
    d = HEAD_DIM
    tok = q_ref.shape[0]

    def stacked(ref):
        return jnp.concatenate([ref[:, r * d : (r + 1) * d] for r in range(group)], axis=0)

    low = jnp.concatenate([low_ref[...]] * group, axis=0)
    pos = jnp.concatenate([pos_ref[...]] * group, axis=0)
    q = stacked(q_ref) * score_scale
    qh, ql = split(q)
    qhl = jnp.concatenate([qh, ql], axis=1)
    top = None
    for j in range(reach1):
        kh, kl = split(k_refs[j][...])
        s = mm(qhl, jnp.concatenate([kh, kh], axis=1), NT) + mm(qh, kl, NT)
        kid = kidx_ref[j : j + 1, :]
        s = jnp.where((kid >= low) & (kid <= pos), s, neg_fill)
        s_ref[j] = s
        m = jnp.max(s, axis=1, keepdims=True)
        top = m if top is None else jnp.maximum(top, m)
    total = jnp.zeros_like(top)
    acc = jnp.zeros((group * tok, d), f32)
    for j in range(reach1):
        p = jnp.exp(s_ref[j] - top)
        total = total + jnp.sum(p, axis=1, keepdims=True)
        ph, plo = split(p)
        ph_ref[j] = ph
        pl_ref[j] = plo
        vh, vl = split(v_refs[j][...])
        both = mm(ph, jnp.concatenate([vh, vl], axis=1), NN)
        acc = acc + (both[:, :d] + both[:, d:]) + mm(plo, vh, NN)
    inv = 1.0 / total
    out = acc * inv
    for r in range(group):
        o_ref[:, r * d : (r + 1) * d] = out[r * tok : (r + 1) * tok]
    grad = stacked(g_ref) * inv
    delta = jnp.sum(grad * out, axis=1, keepdims=True)
    gh, gl = split(grad)
    ghl = jnp.concatenate([gh, gl], axis=1)
    dq = jnp.zeros((group * tok, d), f32)
    for j in range(reach1):
        vh, vl = split(v_refs[j][...])
        kh, kl = split(k_refs[j][...])
        ph, plo = ph_ref[j], pl_ref[j]
        dp = mm(ghl, jnp.concatenate([vh, vh], axis=1), NT) + mm(gh, vl, NT)
        ds = (ph.astype(f32) + plo.astype(f32)) * (dp - delta)
        both = mm(ph, ghl, TN)
        dv_refs[j][...] = both[:, :d] + both[:, d:] + mm(plo, gh, TN)
        sh, sl = split(ds)
        both = mm(sh, qhl, TN)
        dk_refs[j][...] = both[:, :d] + both[:, d:] + mm(sl, qh, TN)
        both = mm(sh, jnp.concatenate([kh, kl], axis=1), NN)
        dq = dq + (both[:, :d] + both[:, d:]) + mm(sl, kh, NN)
    dq = dq * score_scale
    for r in range(group):
        dq_ref[:, r * d : (r + 1) * d] = dq[r * tok : (r + 1) * tok]


def run_attend(low, pos, kidx, q, grad, kv_pieces):
    tok = q.shape[0]
    reach1 = len(kv_pieces)
    kv_cols = kv_pieces[0].shape[1] // 2
    heads = kv_cols // HEAD_DIM
    group = q.shape[1] // kv_cols
    d = HEAD_DIM
    whole = lambda *shape: pl.BlockSpec(shape, lambda h: (0,) * len(shape))
    qspec = pl.BlockSpec((tok, group * d), lambda h: (0, h))
    kspec = pl.BlockSpec((tok, d), lambda h: (0, h))
    vspec = pl.BlockSpec((tok, d), lambda h: (0, h + heads))
    flops = 2 * 6 * 3 * tok * group * tok * reach1 * d * heads
    outs = pl.pallas_call(
        functools.partial(attend, reach1, group),
        grid=(heads,),
        in_specs=[whole(tok, 1), whole(tok, 1), whole(*kidx.shape), qspec, qspec]
        + [kspec] * reach1
        + [vspec] * reach1,
        out_specs=[qspec, qspec] + [kspec] * (2 * reach1),
        out_shape=[jax.ShapeDtypeStruct(q.shape, f32)] * 2
        + [jax.ShapeDtypeStruct((tok, kv_cols), f32)] * (2 * reach1),
        scratch_shapes=[
            pltpu.VMEM((reach1, group * tok, tok), f32),
            pltpu.VMEM((reach1, group * tok, tok), bf16),
            pltpu.VMEM((reach1, group * tok, tok), bf16),
        ],
        compiler_params=pltpu.CompilerParams(vmem_limit_bytes=40 * 2**20),
        cost_estimate=pl.CostEstimate(
            flops=2 * flops, bytes_accessed=4 * (4 * q.size + 20 * tok * kv_cols), transcendentals=0
        ),
    )(low, pos, kidx, q, grad, *kv_pieces, *kv_pieces)
    return outs[0], outs[1], outs[2 : 2 + reach1], outs[2 + reach1 :]


def fused(heads, group, n, positions_ref, q_hbm, k_hbm, v_hbm, g_hbm, o_hbm, dq_hbm, dk_hbm, dv_hbm,
          qb, gb, kv, dkv, ob, dqb, r34, rx, rd, s_ref, ph_ref, pl_ref, low_ref, pos_ref, kidx_ref,
          in_send, in_recv, in_local, up_send, up_recv, cross_send, cross_recv, core_send, core_recv,
          b34_send, b34_recv, bx_send, bx_recv, bd_send, bd_recv, out_send, out_recv, out_local):
    d = HEAD_DIM
    gd = group * d
    s, t = lax.axis_index("seq"), lax.axis_index("tp")
    rows = q_hbm.shape[0]
    c1 = lax.rem(s, 2)
    x1 = lax.rem(s // 2, 2)
    mate = {"tp": 1 - t}
    core = {"seq": s + 1 - 2 * c1}
    cross = {"seq": s + 2 - 4 * x1}
    above = {"seq": lax.rem(s + 4, n)}
    below = {"seq": lax.rem(s + n - 4, n)}
    has_below, has_above = s >= 4, s < n - 4

    barrier = pltpu.get_barrier_semaphore()

    def greet(who):
        pl.semaphore_signal(barrier, inc=1, device_id=who, device_id_type=MESH)

    for who in (mate, core, cross, above, below):
        greet(who)
    pl.semaphore_wait(barrier, 5)

    def remote(a, b, ss, rs, who):
        return pltpu.make_async_remote_copy(
            src_ref=a, dst_ref=b, send_sem=ss, recv_sem=rs, device_id=who, device_id_type=MESH
        )

    def cols(ref, who, h, width):
        start = pl.multiple_of(who * (heads * width) + h * width, width)
        return ref.at[:, pl.ds(start, width)]

    def landing(i, h, half):
        r = pl.ds(half * rows, rows)
        if i == 0:
            return kv.at[h, 0, 0, r, :]
        if i == 1:
            return kv.at[h, 0, 1, r, :]
        return (qb if i == 2 else gb).at[h, r, :]

    in_src = ((k_hbm, d), (v_hbm, d), (q_hbm, gd), (g_hbm, gd))

    def y_in(i, h):
        ref, w = in_src[i]
        return remote(cols(ref, 1 - t, h, w), landing(i, h, 1), in_send.at[i, h], in_recv.at[i, h], mate)

    def l_in(i, h):
        ref, w = in_src[i]
        return pltpu.make_async_copy(cols(ref, t, h, w), landing(i, h, 0), in_local.at[i, h])

    def up(h):
        return remote(kv.at[h, 0], kv.at[h, 1], up_send.at[h], up_recv.at[h], above)

    def over(h):
        return remote(kv.at[h, x1], kv.at[h, 2], cross_send.at[h], cross_recv.at[h], cross)

    def near(i, h):
        a = kv.at[h, c1] if i == 0 else kv.at[h, 2]
        return remote(a, kv.at[h, 3 + i], core_send.at[i, h], core_recv.at[i, h], core)

    def b34(h):
        return remote(dkv.at[h, pl.ds(3, 2)], r34.at[h], b34_send.at[h], b34_recv.at[h], core)

    def bx(h):
        return remote(dkv.at[h, 2], rx.at[h], bx_send.at[h], bx_recv.at[h], cross)

    def bd(h):
        return remote(dkv.at[h, 1], rd.at[h], bd_send.at[h], bd_recv.at[h], below)

    out_dst = ((o_hbm, gd), (dq_hbm, gd), (dk_hbm, d), (dv_hbm, d))

    def leaving(i, h, half):
        r = pl.ds(half * rows, rows)
        if i < 2:
            return (ob if i == 0 else dqb).at[h, r, :]
        return dkv.at[h, 0, i - 2, r, :]

    def y_out(i, h):
        ref, w = out_dst[i]
        return remote(leaving(i, h, 1), cols(ref, t, h, w), out_send.at[i, h], out_recv.at[i, h], mate)

    def l_out(i, h):
        ref, w = out_dst[i]
        return pltpu.make_async_copy(leaving(i, h, 0), cols(ref, t, h, w), out_local.at[i, h])

    def each(body):
        def run(h, carry):
            body(h)
            return carry

        lax.fori_loop(0, heads, run, 0)

    def begin(kinds):
        def body(h):
            for i in kinds:
                y_in(i, h).start()
                l_in(i, h).start()

        each(body)

    begin((0, 1))
    begin((2, 3))

    tok = 2 * rows

    def order(axis, shape):
        i = lax.broadcasted_iota(jnp.int32, shape, axis)
        return lax.rem(i + t * rows, tok)

    half = lambda who: positions_ref[pl.ds(pl.multiple_of(who * rows, rows), rows), :]
    since = jnp.concatenate([half(t), half(1 - t)], axis=0)
    pos = s * tok + order(0, (tok, 1))
    pos_ref[...] = pos
    low_ref[...] = jnp.maximum(jnp.maximum(pos - since, pos - (WINDOW - 1)), 0)
    blocks = (s, s - 4, s - 2, s - 3 + 2 * c1, s - 1 - 2 * c1)
    for j in range(5):
        kidx_ref[j : j + 1, :] = blocks[j] * tok + order(1, (1, tok))

    def stage_a(h):
        for i in (0, 1):
            l_in(i, h).wait()
            y_in(i, h).wait_recv()

        @pl.when(has_above)
        def _():
            up(h).start()

    def stage_b(h):
        @pl.when(has_below)
        def _():
            up(h).wait_recv()

        @pl.when(jnp.logical_not(has_below))
        def _():
            kv[h, 1] = jnp.zeros(kv.shape[2:], f32)

        over(h).start()
        near(0, h).start()

    def stage_c(h):
        over(h).wait_recv()
        near(1, h).start()

    def compute(h):
        for i in (2, 3):
            l_in(i, h).wait()
            y_in(i, h).wait_recv()
        for i in (0, 1):
            near(i, h).wait_recv()
        attend(
            5, group, low_ref, pos_ref, kidx_ref, qb.at[h], gb.at[h],
            *[kv.at[h, j, 0] for j in range(5)],
            *[kv.at[h, j, 1] for j in range(5)],
            ob.at[h], dqb.at[h],
            *[dkv.at[h, j, 0] for j in range(5)],
            *[dkv.at[h, j, 1] for j in range(5)],
            s_ref, ph_ref, pl_ref,
        )
        b34(h).start()
        for i in (0, 1):
            y_out(i, h).start()
            l_out(i, h).start()

    def stage_e2(h):
        b34(h).wait()
        dkv[h, 2] = dkv[h, 2] + r34[h, 1]
        dkv[h, c1] = dkv[h, c1] + r34[h, 0]
        bx(h).start()

    def stage_e3(h):
        bx(h).wait()
        dkv[h, x1] = dkv[h, x1] + rx[h]

        @pl.when(has_below)
        def _():
            bd(h).start()

    def stage_e4(h):
        @pl.when(has_above)
        def _():
            bd(h).wait_recv()
            dkv[h, 0] = dkv[h, 0] + rd[h]

        for i in (2, 3):
            y_out(i, h).start()
            l_out(i, h).start()

    stages = STAGES(stage_a, stage_b, stage_c, compute, stage_e2, stage_e3, stage_e4)
    last = max(lag for lag, _ in stages)

    def step(i, carry):
        for lag, stage in stages:
            @pl.when((i >= lag) & (i < lag + heads))
            def _():
                stage(i - lag)

        return carry

    lax.fori_loop(0, heads + last, step, 0)

    def finish(h):
        for i in range(4):
            y_in(i, h).wait_send()
            y_out(i, h).wait()
            l_out(i, h).wait()
        over(h).wait_send()
        near(0, h).wait_send()
        near(1, h).wait_send()

        @pl.when(has_above)
        def _():
            up(h).wait_send()

        @pl.when(has_below)
        def _():
            bd(h).wait_send()

    each(finish)


def STAGES(a, b, c, compute, e2, e3, e4):
    return ((0, a), (1, b), (2, c), (LEAD, compute), (LEAD + 1, e2), (LEAD + 2, e3), (LEAD + 3, e4))


def run_fused(positions, queries, keys, values, out_grad):
    rows = queries.shape[0]
    tok = 2 * rows
    d = HEAD_DIM
    heads = keys.shape[1] // (2 * d)
    group = queries.shape[1] // keys.shape[1]
    gd = group * d
    n = lax.axis_size("seq")
    vm = pl.BlockSpec(memory_space=pltpu.VMEM)
    hbm = pl.BlockSpec(memory_space=pl.ANY)
    dma = lambda *shape: pltpu.SemaphoreType.DMA(shape)
    flops = 2 * 6 * 3 * tok * group * tok * 5 * d * heads
    return pl.pallas_call(
        functools.partial(fused, heads, group, n),
        in_specs=[vm] + [hbm] * 4,
        out_specs=[hbm] * 4,
        out_shape=[jax.ShapeDtypeStruct(x.shape, f32) for x in (queries, queries, keys, values)],
        scratch_shapes=[
            pltpu.VMEM((heads, tok, gd), f32),
            pltpu.VMEM((heads, tok, gd), f32),
            pltpu.VMEM((heads, 5, 2, tok, d), f32),
            pltpu.VMEM((heads, 5, 2, tok, d), f32),
            pltpu.VMEM((heads, tok, gd), f32),
            pltpu.VMEM((heads, tok, gd), f32),
            pltpu.VMEM((heads, 2, 2, tok, d), f32),
            pltpu.VMEM((heads, 2, tok, d), f32),
            pltpu.VMEM((heads, 2, tok, d), f32),
            pltpu.VMEM((5, group * tok, tok), f32),
            pltpu.VMEM((5, group * tok, tok), bf16),
            pltpu.VMEM((5, group * tok, tok), bf16),
            pltpu.VMEM((tok, 1), jnp.int32),
            pltpu.VMEM((tok, 1), jnp.int32),
            pltpu.VMEM((5, tok), jnp.int32),
            dma(4, heads), dma(4, heads), dma(4, heads),
            dma(heads), dma(heads),
            dma(heads), dma(heads),
            dma(2, heads), dma(2, heads),
            dma(heads), dma(heads),
            dma(heads), dma(heads),
            dma(heads), dma(heads),
            dma(4, heads), dma(4, heads), dma(4, heads),
        ],
        compiler_params=pltpu.CompilerParams(
            vmem_limit_bytes=58 * 2**20, collective_id=0, has_side_effects=True
        ),
        cost_estimate=pl.CostEstimate(flops=flops, bytes_accessed=48 * queries.size, transcendentals=0),
    )(positions[:, None], queries, keys, values, out_grad)


def per_device(queries, keys, values, out_grad, positions):
    seq_size, tp_size = lax.axis_size("seq"), lax.axis_size("tp")
    s = lax.axis_index("seq")
    t = lax.axis_index("tp")
    rows = queries.shape[0]
    tok = rows * tp_size
    if tp_size == 2:
        return tuple(run_fused(positions, queries, keys, values, out_grad))
    kw = keys.shape[1] // tp_size

    def shift_seq(x, route):
        return lax.ppermute(x, "seq", [(a, b) for a, b in route if 0 <= b < seq_size])

    up = [(i, i + 4) for i in range(seq_size)]
    down = [(i, i - 4) for i in range(seq_size)]
    cross = [(i, i ^ 2) for i in range(seq_size)]
    core = [(i, i ^ 1) for i in range(seq_size)]

    local = jnp.arange(tok, dtype=jnp.int32)
    first = s * tok
    pos = first + local
    low = jnp.maximum(jnp.maximum(pos - positions, pos - (WINDOW - 1)), 0)

    b = s % 4
    base = s - b
    x1, c1 = b // 2 == 1, b % 2 == 1
    p2_block = s - 2
    c_p2 = (s ^ 1) - 2
    c_first = jnp.where(c1, s - 1, s - 3)
    blocks = jnp.stack([s, s - 4, p2_block, c_first, c_p2])
    kidx = blocks[:, None] * tok + local[None, :]

    pos, low = pos[:, None], low[:, None]

    a2a = lambda x: lax.all_to_all(x, "tp", split_axis=1, concat_axis=0, tiled=True)
    b2a = lambda x: lax.all_to_all(x, "tp", split_axis=0, concat_axis=1, tiled=True)
    q, grad = a2a(queries), a2a(out_grad)
    own = jnp.concatenate([a2a(keys), a2a(values)], axis=1)
    prior = shift_seq(own, up)
    crossed = shift_seq(jnp.where(x1, prior, own), cross)
    near = shift_seq(jnp.where(c1, prior, own), core)
    near_crossed = shift_seq(crossed, core)
    pieces = [own, prior, crossed, near, near_crossed]
    out, dq, dks, dvs = run_attend(low, pos, kidx, q, grad, pieces)
    g_own, g_prior, g_crossed, g_near, g_nc = [
        jnp.concatenate([dk, dv], axis=1) for dk, dv in zip(dks, dvs)
    ]
    near_back = shift_seq(g_near, core)
    g_crossed = g_crossed + shift_seq(g_nc, core)
    zero = jnp.zeros_like(g_own)
    g_own = g_own + jnp.where(c1, zero, near_back)
    g_prior = g_prior + jnp.where(c1, near_back, zero)
    cross_back = shift_seq(g_crossed, cross)
    g_own = g_own + jnp.where(x1, zero, cross_back)
    g_prior = g_prior + jnp.where(x1, cross_back, zero)
    g_own = g_own + shift_seq(g_prior, down)
    return (b2a(out), b2a(dq), b2a(g_own[:, :kw]), b2a(g_own[:, kw:]))


def solution(mesh):
    spec = P(("seq", "tp"), None)
    return jax.shard_map(
        per_device,
        mesh=mesh,
        in_specs=(spec, spec, spec, spec, P("seq")),
        out_specs=(spec, spec, spec, spec),
        check_vma=False,
    )
```
